32 devices in a mesh: tm: 8 (over z, x), chan: 4 (over y, core).
Axes of the slice: x: 2, y: 2, z: 4, core: 2. Of those that a mesh axis runs over, the one named last changes fastest.
Arguments:
- visibilities: bfloat16 [2, 4096, 16, 2048], P(None, 'tm', 'chan'), may hold values from -24 to 24
- beam_transfer: bfloat16 [2, 16, 2048, 256], P(None, 'chan'), may hold values from -0.125 to 0.125
- sky_modes: bfloat16 [2, 4096, 16, 256], P(None, 'tm', 'chan'), may hold values from -6 to 6
- inverse_gains: float32 [2, 1024], replicated, may hold values from -6 to 6
- phase_rate: float32 [2048], replicated, may hold values from -0.05 to 0.05
- feed_pairs: int32 [2, 2048], replicated, may hold values from 0 to 1023, as said below
- block_owner: int32 [8], replicated, may hold values from 0 to 7, each once
Outputs:
- sky_grad: bfloat16 [2, 4096, 16, 256], P(None, 'tm', 'chan')
- feed_grad: float32 [2, 1024], P(None, 'tm')
The draws below stay inside these ranges and needn't reach their ends.
Inputs may be any that keep to these rules, and one draw needn't show every extreme that they name: The two feeds of a baseline differ; every feed appears in feed_pairs[0]. `block_owner`: each device index appears exactly once.
All inputs are finite; a program needn't handle non-finite values.
Results may differ from the reference program's by a relative error of at most 0.0057.
Values may be sent and summed in bfloat16 or wider, within the bound.
A program may use at most 256 MiB of HBM per device.

```python
import math
import jax
import jax.numpy as jnp
from jax import lax

TIMES = 4096
CH = 16
BASE = 2048
K = 256
FEEDS = 1024
NBLK = 8


def draw_visibilities(key, part):
    key = jax.random.fold_in(key, 11)
    noise_key, scale_key = jax.random.split(key)
    values = jnp.clip(jax.random.normal(noise_key, (2, TIMES, CH, BASE), jnp.float32), -6.0, 6.0)
    spread = jax.random.uniform(scale_key, (1, 1, CH, BASE), jnp.float32, 0.0, math.log(4.0))
    return (values * jnp.exp(spread)).astype(jnp.bfloat16)


def draw_feed_pairs(key, part):
    key = jax.random.fold_in(key, 23)
    order_key, extra_key, offset_key = jax.random.split(key, 3)
    every_feed = jax.random.permutation(order_key, FEEDS).astype(jnp.int32)
    extra_feeds = jax.random.randint(extra_key, (BASE - FEEDS,), 0, FEEDS).astype(jnp.int32)
    feed_first = jnp.concatenate([every_feed, extra_feeds])
    offset = jax.random.randint(offset_key, (BASE,), 1, FEEDS).astype(jnp.int32)
    feed_second = (feed_first + offset) % FEEDS
    return jnp.stack([feed_first, feed_second]).astype(jnp.int32)


def levels(own_key, extent, cuts, least, top_value):
    def one(axis_at, parts):
        draws = jax.random.uniform(jax.random.fold_in(jax.random.fold_in(own_key, 6), axis_at), (parts,), jnp.float32, least / len(cuts), top_value / len(cuts))
        return jnp.repeat(jnp.exp(draws), extent[axis_at] // parts).reshape((-1,) + (1,) * (len(extent) - axis_at - 1))

    loudness = one(*cuts[0])
    for cut in cuts[1:]:
        loudness = loudness * one(*cut)
    return loudness


def scatter_about(own_key, dims, deviation, bound, pieces=(), held_as=jnp.bfloat16):
    loudness = levels(own_key, dims, pieces, -0.22, 0.18) if pieces else 1.0
    result = jax.random.normal(own_key, dims, jnp.float32) * deviation * loudness
    return jnp.minimum(jnp.maximum(result, -bound), bound).astype(held_as)


def setup_inputs(seed: int = 0) -> dict:
    keys = jax.random.split(jax.random.key(seed), 8)
    visibilities = draw_visibilities(jax.random.fold_in(keys[7], 71), 0)
    beam_transfer = scatter_about(keys[1], (2, CH, BASE, K), BASE ** -0.5, 0.125, ((1, 4),))
    sky_modes = scatter_about(keys[2], (2, TIMES, CH, K), 1.0, 6.0, ((1, 8), (2, 4)))
    inverse_gains = scatter_about(keys[3], (2, FEEDS), 1.0, 6.0, (), jnp.float32)
    phase_rate = jnp.clip(jax.random.uniform(keys[4], (BASE,), jnp.float32, -0.05, 0.05), -0.05, 0.05)
    feed_pairs = draw_feed_pairs(jax.random.fold_in(keys[7], 71), 0)
    block_owner = jax.random.permutation(keys[6], NBLK).astype(jnp.int32)
    return dict(visibilities=visibilities, beam_transfer=beam_transfer, sky_modes=sky_modes, inverse_gains=inverse_gains, phase_rate=phase_rate, feed_pairs=feed_pairs, block_owner=block_owner)


def feed_terms(cross_real, cross_imag, feed_first, feed_second, inverse_gains):
    first_gain = inverse_gains[:, feed_first]
    second_gain = inverse_gains[:, feed_second]
    second_real = first_gain[0] * cross_real - first_gain[1] * cross_imag
    second_imag = first_gain[0] * cross_imag + first_gain[1] * cross_real
    first_real = second_gain[0] * cross_real + second_gain[1] * cross_imag
    first_imag = second_gain[1] * cross_real - second_gain[0] * cross_imag
    feed_count = inverse_gains.shape[1]
    summed_real = jax.ops.segment_sum(second_real, feed_second, feed_count) + jax.ops.segment_sum(first_real, feed_first, feed_count)
    summed_imag = jax.ops.segment_sum(second_imag, feed_second, feed_count) + jax.ops.segment_sum(first_imag, feed_first, feed_count)
    return jnp.stack([summed_real, summed_imag])

def reference(visibilities, beam_transfer, sky_modes, inverse_gains, phase_rate, feed_pairs, block_owner):
    block_rows = TIMES // NBLK
    indices = jnp.arange(NBLK, dtype=jnp.int32)
    inverse = lax.optimization_barrier(jnp.sum(jnp.where(block_owner[None, :] == indices[:, None], indices[None, :], 0), axis=1)).astype(jnp.int32)
    order = (inverse[:, None] * block_rows + jnp.arange(block_rows, dtype=jnp.int32)[None, :]).reshape(TIMES)
    turn_angle = order.astype(jnp.float32)[:, None] * phase_rate[None, :]
    cosine_part = jnp.cos(turn_angle)
    sine_part = jnp.sin(turn_angle)
    first_gain = inverse_gains[:, feed_pairs[0]]
    second_gain = inverse_gains[:, feed_pairs[1]]
    pair_real = first_gain[0] * second_gain[0] + first_gain[1] * second_gain[1]
    pair_imag = first_gain[1] * second_gain[0] - first_gain[0] * second_gain[1]

    def channel(channel_index):
        series = visibilities[:, :, channel_index, :].astype(jnp.float32)
        spectrum = jnp.fft.fft(series[0] + 1j * series[1], axis=0) / jnp.sqrt(jnp.float32(TIMES))
        spectrum = spectrum[order]
        stacked = jnp.stack([jnp.real(spectrum), jnp.imag(spectrum)]).astype(jnp.float32)
        rounded = lax.optimization_barrier(stacked.astype(jnp.bfloat16)).astype(jnp.float32)
        rotated_real = cosine_part * rounded[0] + sine_part * rounded[1]
        rotated_imag = cosine_part * rounded[1] - sine_part * rounded[0]
        beam_real = beam_transfer[0, channel_index]
        beam_imag = beam_transfer[1, channel_index]
        sky_real = sky_modes[0, :, channel_index, :]
        sky_imag = sky_modes[1, :, channel_index, :]
        model_real = jnp.dot(sky_real, beam_real.T, preferred_element_type=jnp.float32) - jnp.dot(sky_imag, beam_imag.T, preferred_element_type=jnp.float32)
        model_imag = jnp.dot(sky_real, beam_imag.T, preferred_element_type=jnp.float32) + jnp.dot(sky_imag, beam_real.T, preferred_element_type=jnp.float32)
        misfit_real = (pair_real * rotated_real - pair_imag * rotated_imag - model_real).astype(jnp.bfloat16)
        misfit_imag = (pair_real * rotated_imag + pair_imag * rotated_real - model_imag).astype(jnp.bfloat16)
        grad_real = (jnp.dot(misfit_real, beam_real, preferred_element_type=jnp.float32) + jnp.dot(misfit_imag, beam_imag, preferred_element_type=jnp.float32)).astype(jnp.bfloat16)
        grad_imag = (jnp.dot(misfit_imag, beam_real, preferred_element_type=jnp.float32) - jnp.dot(misfit_real, beam_imag, preferred_element_type=jnp.float32)).astype(jnp.bfloat16)
        filtered_real = jnp.dot(grad_real, beam_real.T, preferred_element_type=jnp.float32) - jnp.dot(grad_imag, beam_imag.T, preferred_element_type=jnp.float32)
        filtered_imag = jnp.dot(grad_real, beam_imag.T, preferred_element_type=jnp.float32) + jnp.dot(grad_imag, beam_real.T, preferred_element_type=jnp.float32)
        cross_real = lax.optimization_barrier(jnp.sum(filtered_real * rotated_real + filtered_imag * rotated_imag, axis=0))
        cross_imag = lax.optimization_barrier(jnp.sum(filtered_real * rotated_imag - filtered_imag * rotated_real, axis=0))
        return (jnp.stack([grad_real, grad_imag]), jnp.stack([cross_real, cross_imag]))
    grads, crosses = lax.map(channel, jnp.arange(CH, dtype=jnp.int32))
    sky_grad = jnp.transpose(grads, (1, 2, 0, 3))
    cross_total = lax.optimization_barrier(jnp.sum(crosses, axis=0))
    grad_scale = 0.25 / (TIMES * CH)
    feed_grad = grad_scale * feed_terms(cross_total[0], cross_total[1], feed_pairs[0], feed_pairs[1], inverse_gains)
    return (sky_grad, feed_grad)
```

```python
import functools
import math

import jax
import jax.numpy as jnp
from jax import lax
from jax.experimental import pallas as pl
from jax.experimental.pallas import tpu as pltpu
from jax.sharding import PartitionSpec as P

F32 = jnp.float32
BF16 = jnp.bfloat16
RADIX = 4
MIB = 1024 * 1024


def transform_kernel(piece, pieces, chunk, owner_ref, series_ref, beam_ref, gain_ref, table_ref, turn_ref, rot_ref, proj_ref, weight_ref, total_ref):
    tile = pl.program_id(0)
    tile_rows = turn_ref.shape[1]
    width = turn_ref.shape[2]
    modes = beam_ref.shape[2]
    block_rows = proj_ref.shape[1]
    span = pl.num_programs(0) * tile_rows

    @pl.when(tile == 0)
    def _():
        def fill(step, carry):
            rows = pl.ds(pl.multiple_of(step * chunk, chunk), chunk)
            real = beam_ref[0, rows, :].astype(F32)
            imag = beam_ref[1, rows, :].astype(F32)
            for part in range(RADIX):
                gain_real = gain_ref[rows, 2 * part : 2 * part + 1]
                gain_imag = gain_ref[rows, 2 * part + 1 : 2 * part + 2]
                out_real = (real * gain_real + imag * gain_imag).astype(BF16)
                out_imag = (real * gain_imag - imag * gain_real).astype(BF16)
                weight_ref[part, 0, rows, :modes] = out_real
                weight_ref[part, 0, rows, modes:] = out_imag
                weight_ref[part, 1, rows, :modes] = -out_imag
                weight_ref[part, 1, rows, modes:] = out_real
            return carry

        lax.fori_loop(0, width // chunk, fill, 0)

    total_ref[...] = jnp.zeros_like(total_ref)

    def work(step, carry):
        cols = pl.ds(pl.multiple_of(step * chunk, chunk), chunk)
        parts = []
        for part in range(RADIX):
            both = jnp.dot(table_ref[0, part], series_ref[0, part, :, cols], preferred_element_type=F32)
            parts.append((both[:tile_rows], both[tile_rows:]))
        (ar, ai), (br, bi), (cr, ci), (dr, di) = parts
        sr, si, er, ei = ar + cr, ai + ci, ar - cr, ai - ci
        tr, ti, fr, fi = br + dr, bi + di, br - dr, bi - di
        outs = ((sr + tr, si + ti), (er + fi, ei - fr), (sr - tr, si - ti), (er - fi, ei + fr))
        turn_real = turn_ref[0, :, cols].astype(F32)
        turn_imag = turn_ref[1, :, cols].astype(F32)
        for part in range(RADIX):
            xr, xi = outs[part]
            zr = (xr * turn_real - xi * turn_imag).astype(BF16)
            zi = (xr * turn_imag + xi * turn_real).astype(BF16)
            rot_ref[0, part, :, cols] = zr
            rot_ref[1, part, :, cols] = zi
            total_ref[part] += jnp.dot(
                zr, weight_ref[part, 0, cols, :], preferred_element_type=F32
            ) + jnp.dot(zi, weight_ref[part, 1, cols, :], preferred_element_type=F32)
        return carry

    lax.fori_loop(0, width // chunk, work, 0)
    for part in range(RADIX):
        for index in range(pieces):
            row = part * span + tile * tile_rows + index * piece
            owner = owner_ref[row // block_rows]
            start = pl.multiple_of(row % block_rows, piece)
            proj_ref[owner, pl.ds(start, piece), :] = total_ref[
                part, index * piece : (index + 1) * piece, :
            ].astype(BF16)


def transform(owner, series, beam, gains, table, turns, block_rows, tile_rows, channel):
    tiles = table.shape[0]
    width = series.shape[3]
    depth = series.shape[2]
    modes = beam.shape[2]
    span = tiles * tile_rows
    blocks = owner.shape[0]
    piece = min(block_rows, tile_rows)
    chunk = 256
    one = pl.Buffered(1)
    return pl.pallas_call(
        functools.partial(transform_kernel, piece, tile_rows // piece, chunk),
        grid=(tiles,),
        in_specs=[
            pl.BlockSpec(memory_space=pltpu.SMEM),
            pl.BlockSpec((1, RADIX, depth, width), lambda t: (channel, 0, 0, 0), pipeline_mode=one),
            pl.BlockSpec((2, width, modes), lambda t: (0, 0, 0), pipeline_mode=one),
            pl.BlockSpec((width, 2 * RADIX), lambda t: (0, 0), pipeline_mode=one),
            pl.BlockSpec((1, RADIX, 2 * tile_rows, depth), lambda t: (t, 0, 0, 0)),
            pl.BlockSpec((2, tile_rows, width), lambda t: (0, t, 0)),
        ],
        out_specs=[
            pl.BlockSpec((2, RADIX, tile_rows, width), lambda t: (0, 0, t, 0)),
            pl.BlockSpec((blocks, block_rows, 2 * modes), lambda t: (0, 0, 0)),
        ],
        out_shape=[
            jax.ShapeDtypeStruct((2, RADIX, span, width), BF16),
            jax.ShapeDtypeStruct((blocks, block_rows, 2 * modes), BF16),
        ],
        scratch_shapes=[
            pltpu.VMEM((RADIX, 2, width, 2 * modes), BF16),
            pltpu.VMEM((RADIX, tile_rows, 2 * modes), F32),
        ],
        compiler_params=pltpu.CompilerParams(vmem_limit_bytes=62 * MIB),
        cost_estimate=pl.CostEstimate(flops=26 * 10**9, bytes_accessed=60 * MIB, transcendentals=0),
        name="transform",
    )(owner, series, beam, gains, table, turns)


def cross_kernel(owner_ref, grad_ref, rot_ref, beam_ref, gain_ref, out_ref):
    blocks, both, block_rows = grad_ref.shape
    modes = both // 2
    per_part = blocks // RADIX
    sum_real = None
    for part in range(RADIX):
        on_real = on_imag = None
        for index in range(per_part):
            grad = grad_ref[owner_ref[part * per_part + index]]
            rows = slice(index * block_rows, (index + 1) * block_rows)
            new_real = jnp.dot(grad, rot_ref[0, part, rows, :], preferred_element_type=F32)
            new_imag = jnp.dot(grad, rot_ref[1, part, rows, :], preferred_element_type=F32)
            on_real = new_real if on_real is None else on_real + new_real
            on_imag = new_imag if on_imag is None else on_imag + new_imag
        wr = on_real[:modes] + on_imag[modes:]
        wi = on_imag[:modes] - on_real[modes:]
        gain_real = gain_ref[2 * part : 2 * part + 1, :]
        gain_imag = gain_ref[2 * part + 1 : 2 * part + 2, :]
        vr = wr * gain_real - wi * gain_imag
        vi = wr * gain_imag + wi * gain_real
        sum_real, sum_imag = (vr, vi) if sum_real is None else (sum_real + vr, sum_imag + vi)
    br = beam_ref[0].astype(F32)
    bi = beam_ref[1].astype(F32)
    out_ref[0:1, :] = jnp.sum(br * sum_real + bi * sum_imag, axis=0, keepdims=True)
    out_ref[1:2, :] = jnp.sum(br * sum_imag - bi * sum_real, axis=0, keepdims=True)


def cross_terms(owner, grads, rot, beam_turned, gains):
    blocks, both, block_rows = grads.shape
    span, width = rot.shape[2], rot.shape[3]
    modes = both // 2
    chunk = 256
    return pl.pallas_call(
        cross_kernel,
        grid=(width // chunk,),
        in_specs=[
            pl.BlockSpec(memory_space=pltpu.SMEM),
            pl.BlockSpec((blocks, both, block_rows), lambda t: (0, 0, 0)),
            pl.BlockSpec((2, RADIX, span, chunk), lambda t: (0, 0, 0, t)),
            pl.BlockSpec((2, modes, chunk), lambda t: (0, 0, t)),
            pl.BlockSpec((2 * RADIX, chunk), lambda t: (0, t)),
        ],
        out_specs=pl.BlockSpec((2, chunk), lambda t: (0, t)),
        out_shape=jax.ShapeDtypeStruct((2, width), F32),
        compiler_params=pltpu.CompilerParams(vmem_limit_bytes=48 * MIB),
        cost_estimate=pl.CostEstimate(flops=17 * 10**9, bytes_accessed=38 * MIB, transcendentals=0),
        name="cross",
    )(owner, grads, rot, beam_turned, gains)


def times(left, right):
    return (left[0] * right[0] - left[1] * right[1], left[0] * right[1] + left[1] * right[0])


def unit(angle):
    return (jnp.cos(angle), -jnp.sin(angle))


def time_tables(position, slab_rows, all_times, tile_rows):
    span = all_times // RADIX
    fine = 32
    scale = 1.0 / math.sqrt(all_times)
    time_index = position * slab_rows + jnp.arange(slab_rows, dtype=jnp.int32)

    def small(step, count):
        index = step * jnp.arange(count, dtype=jnp.int32)[:, None] * time_index[None, :] % all_times
        return unit(index.astype(F32) * (2.0 * math.pi / all_times))

    coarse_part = small(fine, span // fine)
    fine_part = small(1, fine)
    real, imag = times(
        (coarse_part[0][:, None, :] * scale, coarse_part[1][:, None, :] * scale),
        (fine_part[0][None], fine_part[1][None]),
    )
    tiles = span // tile_rows
    depth = slab_rows // RADIX

    def shaped(value):
        return value.reshape(tiles, tile_rows, depth, RADIX).transpose(0, 3, 1, 2)

    real, imag = shaped(real.astype(BF16)), shaped(imag.astype(BF16))
    top = jnp.concatenate([real, -imag], axis=3)
    bottom = jnp.concatenate([imag, real], axis=3)
    return jnp.concatenate([top, bottom], axis=2)


def phase_tables(rates, span):
    fine = 32
    coarse_index = (fine * jnp.arange(span // fine, dtype=jnp.int32)).astype(F32)
    fine_index = jnp.arange(fine, dtype=jnp.int32).astype(F32)
    coarse_part = unit(coarse_index[:, None] * rates[None, :])
    fine_part = unit(fine_index[:, None] * rates[None, :])
    real, imag = times(
        (coarse_part[0][:, None], coarse_part[1][:, None]), (fine_part[0][None], fine_part[1][None])
    )
    turns = jnp.stack([real.astype(BF16), imag.astype(BF16)]).reshape(2, span, rates.shape[0])
    steps = (span * jnp.arange(RADIX, dtype=jnp.int32)).astype(F32)
    return turns, unit(steps[:, None] * rates[None, :])


def body(visibilities, beam_transfer, sky_modes, inverse_gains, phase_rate, feed_pairs, block_owner):
    devices_tm = lax.axis_size("tm")
    position = lax.axis_index("tm")
    slab_rows, channels, width = visibilities.shape[1:]
    modes = beam_transfer.shape[3]
    all_times = slab_rows * devices_tm
    span = all_times // RADIX
    tile_rows = 256
    depth = slab_rows // RADIX

    series = (
        visibilities.reshape(2, depth, RADIX, channels, width)
        .transpose(3, 2, 0, 1, 4)
        .reshape(channels, RADIX, 2 * depth, width)
    )
    table = time_tables(position, slab_rows, all_times, tile_rows)
    turns, steps = phase_tables(phase_rate, span)
    first_gain = inverse_gains[:, feed_pairs[0]]
    second_gain = inverse_gains[:, feed_pairs[1]]
    pair_real = first_gain[0] * second_gain[0] + first_gain[1] * second_gain[1]
    pair_imag = first_gain[1] * second_gain[0] - first_gain[0] * second_gain[1]
    gained = times(steps, (pair_real[None], pair_imag[None]))
    gains_in = jnp.stack(gained, axis=1).reshape(2 * RADIX, width).T
    gains_out = jnp.stack(steps, axis=1).reshape(2 * RADIX, width)

    beam_real, beam_imag = beam_transfer[0], beam_transfer[1]
    product = functools.partial(jnp.einsum, "fbk,fbl->fkl", preferred_element_type=F32)
    gram_real = product(beam_real, beam_real) + product(beam_imag, beam_imag)
    cross_gram = product(beam_real, beam_imag)
    gram_imag = cross_gram - cross_gram.transpose(0, 2, 1)
    beam_turned = beam_transfer.transpose(1, 0, 3, 2)
    gram = jnp.concatenate(
        [
            jnp.concatenate([gram_real, -gram_imag], axis=2),
            jnp.concatenate([gram_imag, gram_real], axis=2),
        ],
        axis=1,
    )
    gram_high = gram.astype(BF16)
    gram_low = (gram - gram_high.astype(F32)).astype(BF16)

    paired = devices_tm == 8
    slots_out = slots_in = block_owner
    if paired:
        half = devices_tm // 2
        side_slot = (block_owner + position) % 2 * half
        slots_out = side_slot + (block_owner // 2 + half - position // 2) % half
        slots_in = side_slot + block_owner // 2
        lines = [[2 * row + side for row in range(half)] for side in range(2)]
        swap = [(index, index ^ 1) for index in range(devices_tm)]

    def pair_reduce(projected):
        if not paired:
            return lax.psum_scatter(
                projected.reshape(all_times, 2 * modes), "tm", scatter_dimension=0, tiled=True
            )
        other = lax.ppermute(projected[half:], "tm", swap)
        return (projected[:half].astype(F32) + other.astype(F32)).astype(BF16)

    def line_reduce(pair_sum):
        if not paired:
            return pair_sum.astype(F32)
        total = pair_sum[0].astype(F32)
        for shift in range(1, half):
            moves = [(index, (index + 2 * shift) % devices_tm) for index in range(devices_tm)]
            total = total + lax.ppermute(pair_sum[shift], "tm", moves).astype(F32)
        return total

    def gather_blocks(grad_turned):
        if not paired:
            return lax.all_gather(grad_turned, "tm", axis=0)
        near = lax.all_gather(grad_turned, "tm", axis=0, axis_index_groups=lines)
        return jnp.concatenate([near, lax.ppermute(near, "tm", swap)])

    def project(channel, series_all, slots):
        beam = lax.dynamic_index_in_dim(beam_transfer, channel, 1, keepdims=False)
        rot, projected = transform(
            slots, series_all, beam, gains_in, table, turns, slab_rows, tile_rows,
            channel if isinstance(channel, int) else 0,
        )
        return rot, pair_reduce(projected)

    def gradient(channel, mine):
        sky = lax.dynamic_index_in_dim(sky_modes, channel, 2, keepdims=False)
        sky = jnp.concatenate([sky[0], sky[1]], axis=1)
        apply = functools.partial(jnp.einsum, "mk,lk->ml", sky, preferred_element_type=F32)
        mine = line_reduce(mine)
        return (mine - (apply(gram_high[channel]) + apply(gram_low[channel]))).astype(BF16)

    def correlate(channel, rot, grad):
        whole = gather_blocks(grad.T)
        return cross_terms(slots_in, whole, rot, beam_turned[channel], gains_out)

    if devices_tm > 8:

        def step(carry, channel):
            one = lax.dynamic_index_in_dim(series, channel, 0)
            rot, mine = project(channel, one, slots_out)
            grad = gradient(channel, mine)
            cross = correlate(channel, rot, grad)
            return carry + cross, grad

        cross, grads = lax.scan(
            step, jnp.zeros((2, width), F32), jnp.arange(channels, dtype=jnp.int32)
        )
    else:
        rots, grads, waits = [], [], []
        for channel in range(channels):
            now = slots_out
            if channel >= 2:
                now, waits[channel - 2] = lax.optimization_barrier((now, waits[channel - 2]))
            if channel >= 3:
                grad = gradient(channel - 3, waits[channel - 3])
                now, grad = lax.optimization_barrier((now, grad))
                grads.append(grad)
            rot, mine = project(channel, series, now)
            rots.append(rot)
            waits.append(mine)
        for channel in range(len(grads), channels):
            grads.append(gradient(channel, waits[channel]))
        cross = sum(correlate(channel, rots[channel], grads[channel]) for channel in range(channels))
        grads = jnp.stack(grads)
    sky_grad = grads.reshape(channels, slab_rows, 2, modes).transpose(2, 1, 0, 3)

    cross = lax.psum(cross, ("tm", "chan"))
    feed_count = inverse_gains.shape[1]
    share = feed_count // devices_tm
    ids = position * share + jnp.arange(share, dtype=jnp.int32)
    on_first = (feed_pairs[0][:, None] == ids[None, :]).astype(F32)
    on_second = (feed_pairs[1][:, None] == ids[None, :]).astype(F32)
    seconds = jnp.stack(times(first_gain, cross))
    firsts = jnp.stack(times(second_gain, (cross[0], -cross[1])))
    gather = functools.partial(jnp.dot, precision=lax.Precision.HIGHEST)
    feed_grad = gather(seconds, on_second) + gather(firsts, on_first)
    grad_scale = 0.25 / (all_times * channels * lax.axis_size("chan"))
    return (sky_grad, feed_grad * grad_scale)


def solution(mesh):
    placed = (
        P(None, "tm", "chan", None),
        P(None, "chan", None, None),
        P(None, "tm", "chan", None),
        P(),
        P(),
        P(),
        P(),
    )
    return jax.shard_map(
        body,
        mesh=mesh,
        in_specs=placed,
        out_specs=(P(None, "tm", "chan", None), P(None, "tm")),
        check_vma=False,
    )
```
